256 devices in a mesh: leaf: 8 (over z), row: 16 (over y, x), col: 2 (over core).
Axes of the slice: x: 4, y: 4, z: 8, core: 2. Of those that a mesh axis runs over, the one named last changes fastest.
Arguments:
- root_inverse: float32 [4096, 4096], P('row', ('leaf', 'col')), as said below
- panel_one: float32 [8, 4096, 2048], P('leaf', 'row', 'col'), may hold values from -0.09375 to 0.09375
- diag_one: float32 [8, 2048, 2048], P('leaf', 'row', 'col'), as said below
- panel_two: float32 [8, 1, 4096, 2048], P('leaf', None, 'row', 'col'), may hold values from -0.09375 to 0.09375
- diag_two: float32 [8, 1, 2048, 2048], P('leaf', None, 'row', 'col'), as said below
- structure: int32 [8, 1, 16], P('leaf'), may hold values from 0 to 23, as said below
Outputs:
- cross_one: float32 [8, 4096, 2048], P('leaf', 'row', 'col')
- inner_one: float32 [8, 2048, 2048], P('leaf', 'row', 'col')
- cross_root: float32 [8, 1, 4096, 2048], P('leaf', None, 'row', 'col')
- cross_sep: float32 [8, 1, 2048, 2048], P('leaf', None, 'row', 'col')
- inner_two: float32 [8, 1, 2048, 2048], P('leaf', None, 'row', 'col')
The draws below stay inside these ranges and needn't reach their ends.
Inputs may be any that keep to these rules, and one draw needn't show every extreme that they name: `structure`: each row of the list holds 16 distinct block numbers in rising order; the first is always 0 and the last always (6144) / 256 - 1. `root_inverse`: Symmetric; diagonal entries of 1 to 3 times positive row and column scales, off-diagonal entries of size about 1 / sqrt(4096). `diag_one`: Symmetric; diagonal entries of 1 to 3 times positive row and column scales, off-diagonal entries of size about 1 / sqrt(2048). `diag_two`: Symmetric; diagonal entries of 1 to 3 times positive row and column scales, off-diagonal entries of size about 1 / sqrt(2048).
All inputs are finite; a program needn't handle non-finite values.
Results may differ from the reference program's by a relative error of at most 0.0003.
Values sent between devices are 32-bit elements; how exact they have to be, the bound alone decides.
No kernel may reach another device: no remote copies, remote signals or barrier semaphores. Data moves between devices by JAX's collectives and lax.ppermute only.
A program may use at most 192 MiB of HBM per device.

```python
import math
import jax
import jax.numpy as jnp
from jax import lax

ROOT = 4096
SEP1 = 2048
SEP2 = 2048
BLK = 256
LISTED = 16
KIDS = 1
N_LEAF = 8


def symmetric(noise, diagonal, order):
    off_part = (noise + jnp.swapaxes(noise, -1, -2)) * (0.5 / math.sqrt(order))
    identity = jnp.eye(order, dtype=jnp.float32)
    matrix = off_part * (1.0 - identity) + identity * diagonal[..., None]
    return matrix


def draw_root_inverse(key, part):
    key = jax.random.fold_in(key, 1)
    first, second = jax.random.split(key, 2)
    noise = jax.random.normal(first, (ROOT, ROOT), jnp.float32)
    diagonal = jax.random.uniform(second, (ROOT,), jnp.float32, 1.0, 3.0)
    return symmetric(noise, diagonal, ROOT)


def draw_diag_one(key, part):
    key = jax.random.fold_in(key, 2)
    first, second = jax.random.split(key, 2)
    noise = jax.random.normal(first, (N_LEAF, SEP1, SEP1), jnp.float32)
    diagonal = jax.random.uniform(second, (N_LEAF, SEP1), jnp.float32, 1.0, 3.0)
    return symmetric(noise, diagonal, SEP1)


def draw_diag_two(key, part):
    key = jax.random.fold_in(key, 3)
    first, second = jax.random.split(key, 2)
    noise = jax.random.normal(first, (N_LEAF, KIDS, SEP2, SEP2), jnp.float32)
    diagonal = jax.random.uniform(second, (N_LEAF, KIDS, SEP2), jnp.float32, 1.0, 3.0)
    return symmetric(noise, diagonal, SEP2)


def draw_structure(key, part):
    key = jax.random.fold_in(key, 4)
    blocks_total = (ROOT + SEP1) // BLK
    keys = jax.random.split(key, N_LEAF * KIDS)
    middle = jax.vmap(lambda single: jax.random.permutation(single, blocks_total - 2)[:LISTED - 2] + 1)(keys)
    middle = jnp.sort(middle.astype(jnp.int32), axis=-1)
    first = jnp.zeros((N_LEAF * KIDS, 1), jnp.int32)
    final = jnp.full((N_LEAF * KIDS, 1), blocks_total - 1, jnp.int32)
    listing = jnp.concatenate([first, middle, final], axis=1)
    return listing.reshape(N_LEAF, KIDS, LISTED).astype(jnp.int32)


def levels(own_key, dims, shards, smallest, top_value):
    factor_of = 1.0
    for position, parts in shards:
        steps = jax.random.uniform(jax.random.fold_in(jax.random.fold_in(own_key, 6), position), (parts,), jnp.float32, smallest / len(shards), top_value / len(shards))
        factor_of = factor_of * jnp.repeat(jnp.exp(steps), dims[position] // parts).reshape((-1,) + (1,) * (len(dims) - 1 - position))
    return factor_of


def centred(stream_key, shape, scale, bound, cuts=(), kind=jnp.bfloat16):
    drawn = scale * jax.random.normal(stream_key, shape, jnp.float32)
    if cuts:
        drawn = drawn * levels(stream_key, shape, cuts, -0.22, 0.18)
    return jnp.clip(drawn, -bound, bound).astype(kind)


def setup_inputs(seed: int = 0) -> dict:
    splits = jax.random.split(jax.random.key(seed), 7)
    return {
        "root_inverse": draw_root_inverse(jax.random.fold_in(splits[6], 71), 0),
        "panel_one": centred(splits[1], (N_LEAF, ROOT, SEP1), ROOT ** -0.5, 0.09375, ((0, 8), (1, 16), (2, 2)), jnp.float32),
        "diag_one": draw_diag_one(jax.random.fold_in(splits[6], 71), 0),
        "panel_two": centred(splits[3], (N_LEAF, KIDS, LISTED * BLK, SEP2), (LISTED * BLK) ** -0.5, 0.09375, ((0, 8), (2, 16), (3, 2)), jnp.float32),
        "diag_two": draw_diag_two(jax.random.fold_in(splits[6], 71), 0),
        "structure": draw_structure(jax.random.fold_in(splits[6], 71), 0),
    }


def exact_dot(left, right):
    return jnp.dot(left, right, precision=lax.Precision.HIGHEST, preferred_element_type=jnp.float32)


def reference(root_inverse, panel_one, diag_one, panel_two, diag_two, structure):
    def one_group(items):
        upper, diag_up, lowers, diag_lows, blocks_all = items
        cross = -exact_dot(root_inverse, upper)
        inner = diag_up - exact_dot(cross.T, upper)
        ancestor = jnp.concatenate([jnp.concatenate([root_inverse, cross], axis=1), jnp.concatenate([cross.T, inner], axis=1)], axis=0)
        roots, seps, inners = [], [], []
        for kid in range(KIDS):
            blocks = blocks_all[kid].astype(jnp.int32)
            rows = (blocks[:, None] * BLK + jnp.arange(BLK, dtype=jnp.int32)[None, :]).reshape(-1).astype(jnp.int32)
            column = -exact_dot(jnp.take(ancestor, rows, axis=1), lowers[kid])
            roots.append(column[:ROOT])
            seps.append(column[ROOT:])
            inners.append(diag_lows[kid] - exact_dot(jnp.take(column, rows, axis=0).T, lowers[kid]))
        return cross, inner, jnp.stack(roots), jnp.stack(seps), jnp.stack(inners)

    cross_one, inner_one, cross_root, cross_sep, inner_two = lax.map(one_group, (panel_one, diag_one, panel_two, diag_two, structure))
    return (cross_one, inner_one, cross_root, cross_sep, inner_two)
```

```python
import jax
import jax.numpy as jnp
from jax import lax
from jax.sharding import PartitionSpec as P

BLK = 256
SIDE = 4


def dot(left, right):
    return jnp.dot(left, right, precision=lax.Precision.HIGH, preferred_element_type=jnp.float32)


def contract_rows(left, right):
    return lax.dot_general(
        left,
        right,
        (((0,), (0,)), ((), ())),
        precision=lax.Precision.HIGH,
        preferred_element_type=jnp.float32,
    )


def pull(value, down, right):
    pairs = []
    for target in range(SIDE * SIDE):
        y, x = divmod(target, SIDE)
        pairs.append((((y + down) % SIDE) * SIDE + (x + right) % SIDE, target))
    return lax.ppermute(value, "row", pairs)


def other_core(value):
    return lax.ppermute(value, "col", [(0, 1), (1, 0)])


def join_cores(mine, axis):
    theirs = other_core(mine)
    first = lax.axis_index("col") == 0
    return jnp.concatenate([jnp.where(first, mine, theirs), jnp.where(first, theirs, mine)], axis=axis)


def gather_rounds(own):
    got = {(0, 0): own}
    rounds = [[(0, 0)]]
    for down, right in ((0, 1), (0, 3), (1, 0), (3, 0)):
        got[down, right] = pull(own, down, right)
    rounds.append([(0, 1), (0, 3), (1, 0), (3, 0)])
    got[1, 1] = pull(got[1, 0], 0, 1)
    got[3, 3] = pull(got[3, 0], 0, 3)
    got[1, 3] = pull(got[0, 3], 1, 0)
    got[3, 1] = pull(got[0, 1], 3, 0)
    rounds.append([(1, 1), (3, 3), (1, 3), (3, 1)])
    got[1, 2] = pull(got[1, 1], 0, 1)
    got[3, 2] = pull(got[3, 3], 0, 3)
    got[2, 1] = pull(got[1, 1], 1, 0)
    got[2, 3] = pull(got[3, 3], 3, 0)
    rounds.append([(1, 2), (3, 2), (2, 1), (2, 3)])
    half, quarter = own.shape[0] // 2, own.shape[0] // 4
    east = pull(jnp.concatenate([got[0, 1][:half], got[2, 1][:quarter]]), 0, 1)
    west = pull(jnp.concatenate([got[0, 3][half:], got[2, 3][quarter:half]]), 0, 3)
    south = pull(jnp.concatenate([got[1, 0][:half], got[1, 2][half:half + quarter]]), 1, 0)
    north = pull(jnp.concatenate([got[3, 0][half:], got[3, 2][half + quarter:]]), 3, 0)
    got[0, 2] = jnp.concatenate([east[:half], west[:half]])
    got[2, 0] = jnp.concatenate([south[:half], north[:half]])
    got[2, 2] = jnp.concatenate([east[half:], west[half:], south[half:], north[half:]])
    rounds.append([(0, 2), (2, 0), (2, 2)])
    return got, rounds


def body(root_inverse, panel_one, diag_one, panel_two, diag_two, structure):
    place = lax.axis_index("row")
    core = lax.axis_index("col")
    down, right = place // SIDE, place % SIDE

    def absolute(spot):
        return ((down + spot[0]) % SIDE) * SIDE + (right + spot[1]) % SIDE

    root_rows = lax.all_gather(root_inverse, ("leaf", "col"), axis=1, tiled=True)
    upper, rounds = gather_rounds(panel_one[0])
    cross = None
    for spots in rounds:
        columns = [lax.dynamic_slice_in_dim(root_rows, absolute(s) * BLK, BLK, axis=1) for s in spots]
        term = dot(jnp.concatenate(columns, axis=1), jnp.concatenate([upper[s] for s in spots], axis=0))
        cross = -term if cross is None else cross - term

    lower_own = panel_two[0, 0] + upper[1, 2][:1, :1] * 0.0
    lower, rounds = gather_rounds(lower_own)

    cross_full = join_cores(cross, 1)
    rows = cross_full.shape[0] // 2
    sent = lax.dynamic_slice_in_dim(cross_full, core * rows, rows, axis=0)
    turned = lax.all_to_all(sent.reshape(rows, SIDE * SIDE, -1), "row", split_axis=1, concat_axis=1, tiled=True)
    turned = join_cores(jnp.swapaxes(turned, 0, 1), 1)
    turned = turned.reshape(-1, turned.shape[-1])
    order = [s for spots in rounds for s in spots]
    upper_all = jnp.concatenate([upper[s] for s in order], axis=0)
    turned_here = jnp.concatenate(
        [lax.dynamic_slice_in_dim(turned, absolute(s) * BLK, BLK, axis=0) for s in order], axis=0
    )
    inner = diag_one[0] - contract_rows(turned_here, upper_all)
    inner_full = join_cores(inner, 1)

    ancestor = jnp.concatenate(
        [
            jnp.concatenate([root_rows, cross_full], axis=1),
            jnp.concatenate([turned.T, inner_full], axis=1),
        ],
        axis=0,
    )
    blocks = structure[0, 0]
    listed = {s: lax.dynamic_index_in_dim(blocks, absolute(s), keepdims=False) for s in order}
    column = None
    for spots in rounds:
        columns = [lax.dynamic_slice_in_dim(ancestor, listed[s] * BLK, BLK, axis=1) for s in spots]
        term = dot(jnp.concatenate(columns, axis=1), jnp.concatenate([lower[s] for s in spots], axis=0))
        column = -term if column is None else column - term

    rows = column.shape[0] // 2
    mine = lax.dynamic_slice_in_dim(column, core * rows, rows, axis=0)
    theirs = other_core(lax.dynamic_slice_in_dim(column, (1 - core) * rows, rows, axis=0))
    first = core == 0
    sent = jnp.concatenate([jnp.where(first, mine, theirs), jnp.where(first, theirs, mine)], axis=1)
    back = lax.all_to_all(sent.reshape(rows, SIDE * SIDE, -1), "row", split_axis=1, concat_axis=1, tiled=True)
    back = join_cores(jnp.swapaxes(back, 0, 1), 1)
    own_root = root_rows.shape[0]
    width = back.shape[-1]
    natural = jnp.concatenate([back[:, :own_root].reshape(-1, width), back[:, own_root:].reshape(-1, width)], axis=0)
    lower_all = jnp.concatenate([lower[s] for s in order], axis=0)
    chosen = jnp.concatenate(
        [lax.dynamic_slice_in_dim(natural, listed[s] * BLK, BLK, axis=0) for s in order], axis=0
    )
    inner_low = diag_two[0, 0] - contract_rows(chosen, lower_all)
    return (
        cross[None],
        inner[None],
        column[None, None, :own_root],
        column[None, None, own_root:],
        inner_low[None, None],
    )


def solution(mesh):
    in_specs = (
        P("row", ("leaf", "col")),
        P("leaf", "row", "col"),
        P("leaf", "row", "col"),
        P("leaf", None, "row", "col"),
        P("leaf", None, "row", "col"),
        P("leaf", None, None),
    )
    out_specs = (
        P("leaf", "row", "col"),
        P("leaf", "row", "col"),
        P("leaf", None, "row", "col"),
        P("leaf", None, "row", "col"),
        P("leaf", None, "row", "col"),
    )
    return jax.shard_map(body, mesh=mesh, in_specs=in_specs, out_specs=out_specs, check_vma=False)
```

```python
import functools

import jax
import jax.numpy as jnp
from jax import lax
from jax.experimental import pallas as pl
from jax.experimental.pallas import tpu as pltpu
from jax.sharding import PartitionSpec as P

BLK = 256
LANES = 128
SIDE = 4
CHIPS = SIDE * SIDE
TILE = 512
VMEM_LIMIT = 60 * 1024 * 1024
EAST, WEST, SOUTH, NORTH = (0, 1), (0, 3), (1, 0), (3, 0)


def split(value):
    high = value.astype(jnp.bfloat16)
    return high, (value - high.astype(jnp.float32)).astype(jnp.bfloat16)


def mxu(left, right):
    return jnp.dot(left, right, preferred_element_type=jnp.float32)


def three_pass(left_high, left_low, rights, widths):
    total, at = None, 0
    for ref, width in zip(rights, widths):
        for start in range(0, width, BLK):
            size = min(BLK, width - start)
            high, low = split(ref[start:start + size, :])
            ours = left_high[:, at:at + size]
            term = mxu(ours, high) + mxu(ours, low) + mxu(left_low[:, at:at + size], high)
            total = term if total is None else total + term
            at += size
    return total


def right_specs(rights):
    return [pl.BlockSpec((array.shape[0], TILE), lambda n, spots: (0, n)) for array in rights]


def call(kernel, columns, in_specs, out_specs, out_shape, scratch, flops, operands):
    return pl.pallas_call(
        kernel,
        grid_spec=pltpu.PrefetchScalarGridSpec(
            num_scalar_prefetch=1,
            grid=(columns // TILE,),
            in_specs=in_specs,
            out_specs=out_specs,
            scratch_shapes=scratch,
        ),
        out_shape=out_shape,
        compiler_params=pltpu.CompilerParams(vmem_limit_bytes=VMEM_LIMIT),
        cost_estimate=pl.CostEstimate(flops=1000, bytes_accessed=1000, transcendentals=0),
    )(*operands)


def cross_kernel(widths, has_base, spots, *refs):
    count = len(widths)
    lefts, rights, rest = refs[:count], refs[count:2 * count], refs[2 * count:]
    base = rest[0] if has_base else None
    out, left_high, left_low = rest[-3:]

    @pl.when(pl.program_id(0) == 0)
    def _():
        at = 0
        for ref, width in zip(lefts, widths):
            left_high[:, at:at + width], left_low[:, at:at + width] = split(ref[...])
            at += width

    total = three_pass(left_high, left_low, rights, widths)
    out[...] = base[...] - total if has_base else -total


def cross_sum(base, left, spots, rights):
    rows, columns = left.shape[0], rights[0].shape[1]
    widths = tuple(array.shape[0] for array in rights)
    tile = pl.BlockSpec((rows, TILE), lambda n, spots: (0, n))
    in_specs = [
        pl.BlockSpec((rows, width), functools.partial(lambda j, n, spots: (0, spots[j]), j))
        for j, width in enumerate(widths)
    ] + right_specs(rights)
    operands = [spots] + [left] * len(rights) + list(rights)
    if base is not None:
        in_specs.append(tile)
        operands.append(base)
    return call(
        functools.partial(cross_kernel, widths, base is not None),
        columns,
        in_specs,
        tile,
        jax.ShapeDtypeStruct((rows, columns), jnp.float32),
        [pltpu.VMEM((rows, sum(widths)), jnp.bfloat16)] * 2,
        6 * rows * columns * sum(widths),
        operands,
    )


def pack_kernel(core, mine, theirs, out):
    ours = pl.program_id(0) == core[0]
    for k in range(out.shape[0]):
        at = slice(k * LANES, (k + 1) * LANES)
        out[k] = jnp.where(ours, mine[:, at], theirs[:, at])


def pack(core, mine, theirs):
    rows, columns = mine.shape[0] // 2, mine.shape[1]
    half = pl.BlockSpec((rows, columns), lambda g, core: (core[0], 0))
    return pl.pallas_call(
        pack_kernel,
        grid_spec=pltpu.PrefetchScalarGridSpec(
            num_scalar_prefetch=1,
            grid=(2,),
            in_specs=[half, half],
            out_specs=pl.BlockSpec((columns // LANES, rows, LANES), lambda g, core: (g, 0, 0)),
        ),
        out_shape=jax.ShapeDtypeStruct((2 * columns // LANES, rows, LANES), jnp.float32),
        compiler_params=pltpu.CompilerParams(vmem_limit_bytes=VMEM_LIMIT),
        cost_estimate=pl.CostEstimate(flops=1000, bytes_accessed=1000, transcendentals=0),
    )(core, mine, theirs)


def in_order(is_first, mine, theirs):
    return jnp.where(is_first, mine, theirs), jnp.where(is_first, theirs, mine)


def inner_kernel(pieces, widths, listed, spots, mine, theirs, *refs):
    rights, base = refs[:len(widths)], refs[len(widths)]
    out, left_high, left_low = refs[-3:]

    @pl.when(pl.program_id(0) == 0)
    def _():
        is_first = spots[len(pieces)] == 0
        at = 0
        for j, halves in enumerate(pieces):
            spot = spots[j]
            chip = jnp.minimum(spot, CHIPS - 1)
            both = in_order(is_first, mine[chip, :LANES, :], theirs[chip, :LANES, :])
            if listed:
                first_low = jnp.clip(2 * (spot - CHIPS), 0, CHIPS - 2)
                lower = [
                    jnp.concatenate(in_order(is_first, mine[chip_low, LANES:, :], theirs[chip_low, LANES:, :]))
                    for chip_low in (first_low, first_low + 1)
                ]
                both = [jnp.where(spot < CHIPS, top, low) for top, low in zip(both, lower)]
            for half in halves:
                left_high[:, at:at + LANES], left_low[:, at:at + LANES] = split(both[half].T)
                at += LANES

    out[...] = base[...] - three_pass(left_high, left_low, rights, widths)


def inner_sum(base, mine, theirs, spots, pieces, rights, listed):
    columns = base.shape[1]
    widths = tuple(array.shape[0] for array in rights)
    whole = pl.BlockSpec(mine.shape, lambda n, spots: (0, 0, 0))
    tile = pl.BlockSpec((base.shape[0], TILE), lambda n, spots: (0, n))
    return call(
        functools.partial(inner_kernel, pieces, widths, listed),
        columns,
        [whole, whole] + right_specs(rights) + [tile],
        tile,
        jax.ShapeDtypeStruct(base.shape, jnp.float32),
        [pltpu.VMEM((base.shape[0], sum(widths)), jnp.bfloat16)] * 2,
        6 * base.shape[0] * columns * sum(widths),
        [spots, mine, theirs] + list(rights) + [base],
    )


def pick_kernel(groups, spots, root, cross_mine, cross_theirs, turned_mine, turned_theirs, mine, theirs, *outs):
    top = root.shape[0]
    count = sum(len(group) for group in groups)
    core = spots[count]
    is_first = core == 0
    j = 0
    for number, group in enumerate(groups):
        high, low = outs[2 * number], outs[2 * number + 1]
        at = 0
        for halves in group:
            spot = spots[j]
            j += 1
            for half in halves:

                def store(upper, lower, at=at):
                    high[:top, at:at + LANES], low[:top, at:at + LANES] = split(upper)
                    high[top:, at:at + LANES], low[top:, at:at + LANES] = split(lower)

                @pl.when(spot < CHIPS)
                def _():
                    columns = pl.ds(pl.multiple_of(spot * BLK + half * LANES, LANES), LANES)
                    turned = in_order(is_first, turned_mine[spot], turned_theirs[spot])[half]
                    store(root[:, columns], turned.T)

                @pl.when(spot >= CHIPS)
                def _():
                    block = spot - CHIPS
                    per_core = cross_mine.shape[1] // BLK
                    ours = block // per_core == core
                    columns = pl.ds(pl.multiple_of((block % per_core) * BLK + half * LANES, LANES), LANES)
                    store(
                        jnp.where(ours, cross_mine[:, columns], cross_theirs[:, columns]),
                        jnp.where(ours, mine[:, columns], theirs[:, columns]),
                    )

                at += LANES


def pick(spots, groups, operands):
    rows = operands[0].shape[0] + operands[-1].shape[0]
    shapes = []
    for group in groups:
        depth = LANES * sum(len(halves) for halves in group)
        shapes += [jax.ShapeDtypeStruct((rows, depth), jnp.bfloat16)] * 2
    space = pl.BlockSpec(memory_space=pltpu.VMEM)
    return pl.pallas_call(
        functools.partial(pick_kernel, groups),
        in_specs=[pl.BlockSpec(memory_space=pltpu.SMEM)] + [space] * len(operands),
        out_specs=[space] * len(shapes),
        out_shape=shapes,
        compiler_params=pltpu.CompilerParams(vmem_limit_bytes=VMEM_LIMIT),
        cost_estimate=pl.CostEstimate(flops=1000, bytes_accessed=1000, transcendentals=0),
    )(spots, *operands)


def column_kernel(widths, core, left_high, left_low, *refs):
    rights, (out_top, out_low, *turning) = refs[:len(widths)], refs[len(widths):]
    total = three_pass(left_high, left_low, rights, widths)
    top = out_top.shape[0]
    out_top[...] = -total[:top]
    out_low[...] = -total[top:]
    for ref, half in zip(turning, (core[0], 1 - core[0])):
        for k in range(TILE // LANES):
            columns = slice(k * LANES, (k + 1) * LANES)
            ref[k, :LANES] = out_top[pl.ds(pl.multiple_of(half * LANES, LANES), LANES), columns]
            ref[k, LANES:] = out_low[pl.ds(pl.multiple_of(half * (LANES // 2), LANES // 2), LANES // 2), columns]


def column_sum(core, left, rights):
    rows, depth = left[0].shape
    columns = rights[0].shape[1]
    top, low = BLK, rows - BLK
    widths = tuple(array.shape[0] for array in rights)
    whole = pl.BlockSpec((rows, depth), lambda n, core: (0, 0))
    tiles = [pl.BlockSpec((size, TILE), lambda n, core: (0, n)) for size in (top, low)]
    turning = pl.BlockSpec((TILE // LANES, rows // 2, LANES), lambda n, core: (n, 0, 0))
    shapes = [jax.ShapeDtypeStruct((size, columns), jnp.float32) for size in (top, low)]
    shapes += [jax.ShapeDtypeStruct((columns // LANES, rows // 2, LANES), jnp.float32)] * 2
    return call(
        functools.partial(column_kernel, widths),
        columns,
        [whole, whole] + right_specs(rights),
        tiles + [turning, turning],
        shapes,
        [],
        6 * rows * columns * depth,
        [core, *left, *rights],
    )


def after(value, *others):
    return lax.optimization_barrier((value,) + others)[0]


def pull(value, way):
    pairs = []
    for target in range(CHIPS):
        y, x = divmod(target, SIDE)
        pairs.append((((y + way[0]) % SIDE) * SIDE + (x + way[1]) % SIDE, target))
    return lax.ppermute(value, "row", pairs)


def other_core(value):
    return lax.ppermute(value, "col", [(0, 1), (1, 0)])


def first_round(own):
    return [pull(own, way) for way in (EAST, WEST, SOUTH, NORTH)]


def second_round(near, *gates):
    e, w, s, n = near
    es = pull(after(s, e, *gates), EAST)
    wn = pull(after(n, w, *gates), WEST)
    sw = pull(after(w, s, *gates), SOUTH)
    ne = pull(after(e, n, *gates), NORTH)
    return es, wn, sw, ne


def third_round(diagonal, *gates):
    es, wn, sw, ne = diagonal
    ees = pull(after(es, *gates), EAST)
    wwn = pull(after(wn, *gates), WEST)
    sse = pull(after(es, sw, *gates), SOUTH)
    nnw = pull(after(wn, ne, *gates), NORTH)
    return ees, wwn, sse, nnw


def fourth_round(near, third, *gates):
    e, w, s, n = near
    ees, wwn, sse, nnw = third
    half = e.shape[0] // 2
    first = pull(after(nnw[:half], wwn, *gates), WEST)
    second = pull(after(wwn[half:], nnw, *gates), NORTH)
    return pull(after(e, ees, *gates), EAST), pull(after(s, sse, *gates), SOUTH), first, second


PLACES = [
    [(0, 0), EAST, WEST, SOUTH, NORTH, (1, 1), (3, 3), (1, 3), (3, 1)],
    [(1, 2), (3, 2), (2, 1), (2, 3)],
    [(0, 2), (2, 0), (2, 2), (2, 2)],
]
WHOLE = (0, 1)
HALVES = [[WHOLE] * 9, [WHOLE] * 4, [WHOLE, WHOLE, (0,), (1,)]]


def body(root_inverse, panel_one, diag_one, panel_two, diag_two, structure):
    place = lax.axis_index("row")
    core = lax.axis_index("col").astype(jnp.int32)
    core_vector = core[None]
    blocks = structure[0, 0]
    own_upper, own_lower = panel_one[0], panel_two[0, 0]

    def chips(places):
        down = jnp.array([spot[0] for spot in places], jnp.int32)
        right = jnp.array([spot[1] for spot in places], jnp.int32)
        return ((place // SIDE + down) % SIDE) * SIDE + (place % SIDE + right) % SIDE

    halves = sum(HALVES, [])
    chip_spots = jnp.concatenate([chips(sum(PLACES, [])), core_vector])
    listed_spots = jnp.concatenate([blocks, core_vector])
    natural = [WHOLE] * blocks.shape[0]
    late_spots = chips(PLACES[1] + PLACES[2])
    scale = jnp.array([1] * 6 + [2, 2], jnp.int32)
    late_spots = late_spots * scale + jnp.array([0] * 7 + [1], jnp.int32)

    root_rows = lax.all_gather(root_inverse, ("leaf", "col"), axis=1, tiled=True)

    near = first_round(own_upper)
    diagonal = second_round(near)
    third = third_round(diagonal)
    lower = lax.all_gather(after(own_lower, *near), "row", axis=0, tiled=True)
    early = [own_upper, *near, *diagonal]
    cross = cross_sum(None, root_rows, chips(PLACES[0]), early)
    fourth = fourth_round(near, third)
    upper = [*early, *third, *fourth]
    cross = cross_sum(cross, root_rows, late_spots, [*third, *fourth])
    cross_theirs = other_core(cross)
    sent = pack(core_vector, cross, cross_theirs)
    turned = lax.all_to_all(sent, "row", split_axis=0, concat_axis=0, tiled=True)
    turned_theirs = other_core(turned)
    inner = inner_sum(diag_one[0], turned, turned_theirs, chip_spots, halves, upper, False)
    inner_theirs = other_core(inner)

    picked = pick(
        listed_spots, [natural], (root_rows, cross, cross_theirs, turned, turned_theirs, inner, inner_theirs)
    )
    top, low, keep, give = column_sum(core_vector, picked, [lower])

    theirs = other_core(give)
    sent = jnp.concatenate(in_order(core == 0, keep, theirs), axis=0)
    turned = lax.all_to_all(sent, "row", split_axis=0, concat_axis=0, tiled=True)
    inner_low = inner_sum(diag_two[0, 0], turned, other_core(turned), listed_spots, natural, [lower], True)
    return cross[None], inner[None], top[None, None], low[None, None], inner_low[None, None]


def solution(mesh):
    in_specs = (
        P("row", ("leaf", "col")),
        P("leaf", "row", "col"),
        P("leaf", "row", "col"),
        P("leaf", None, "row", "col"),
        P("leaf", None, "row", "col"),
        P("leaf", None, None),
    )
    out_specs = (
        P("leaf", "row", "col"),
        P("leaf", "row", "col"),
        P("leaf", None, "row", "col"),
        P("leaf", None, "row", "col"),
        P("leaf", None, "row", "col"),
    )
    return jax.shard_map(body, mesh=mesh, in_specs=in_specs, out_specs=out_specs, check_vma=False)
```

```python
import functools

import jax
import jax.numpy as jnp
from jax import lax
from jax.experimental import pallas as pl
from jax.experimental.pallas import tpu as pltpu
from jax.sharding import PartitionSpec as P

BLK = 256
LANES = 128
SIDE = 4
CHIPS = SIDE * SIDE
TILE = 512
GROUP = 4
PER_CORE = 4
VMEM_LIMIT = 60 * 1024 * 1024
EAST, WEST, SOUTH, NORTH = (0, 1), (0, 3), (1, 0), (3, 0)


def split(value):
    high = value.astype(jnp.bfloat16)
    return high, (value - high.astype(jnp.float32)).astype(jnp.bfloat16)


def mxu(left, right):
    return jnp.dot(left, right, preferred_element_type=jnp.float32)


def three_pass(left_high, left_low, rights, widths):
    total, at = None, 0
    for ref, width in zip(rights, widths):
        for start in range(0, width, BLK):
            size = min(BLK, width - start)
            high, low = split(ref[start:start + size, :])
            ours = left_high[:, at:at + size]
            term = mxu(ours, high) + mxu(ours, low) + mxu(left_low[:, at:at + size], high)
            total = term if total is None else total + term
            at += size
    return total


def stacked_pass(left, rights, widths):
    rows = left.shape[0] // 2
    total, at = None, 0
    for ref, width in zip(rights, widths):
        for start in range(0, width, BLK):
            size = min(BLK, width - start)
            high, low = split(ref[start:start + size, :])
            both = mxu(left[:, at:at + size], high)
            term = both[:rows] + both[rows:] + mxu(left[:rows, at:at + size], low)
            total = term if total is None else total + term
            at += size
    return total


def cross_kernel(widths, has_base, has_turn, spots, core, *refs):
    count = len(widths)
    lefts, rights, rest = refs[:count], refs[count:2 * count], refs[2 * count:]
    base = rest[0] if has_base else None
    out, *turning, left_high, left_low = rest[1:] if has_base else rest

    @pl.when(pl.program_id(0) == 0)
    def _():
        at = 0
        for ref, width in zip(lefts, widths):
            left_high[:, at:at + width], left_low[:, at:at + width] = split(ref[...])
            at += width

    total = three_pass(left_high, left_low, rights, widths)
    out[...] = base[...] - total if has_base else -total
    if has_turn:
        halves_of(out, core[0], *turning)


def cross_sum(base, left, spots, core, rights, has_turn=False):
    rows, columns = left.shape[0], rights[0].shape[1]
    widths = tuple(array.shape[0] for array in rights)
    tile = pl.BlockSpec((rows, TILE), lambda n, spots, core: (0, n))
    in_specs = [
        pl.BlockSpec((rows, width), functools.partial(lambda j, n, spots, core: (0, spots[j]), j))
        for j, width in enumerate(widths)
    ] + [pl.BlockSpec((width, TILE), lambda n, spots, core: (0, n)) for width in widths]
    operands = [spots, core] + [left] * len(rights) + list(rights)
    if base is not None:
        in_specs.append(tile)
        operands.append(base)
    out_specs, shapes = [tile], [(rows, columns)]
    if has_turn:
        out_specs += [pl.BlockSpec((TILE // LANES, rows // 2, LANES), lambda n, spots, core: (n, 0, 0))] * 2
        shapes += [(columns // LANES, rows // 2, LANES)] * 2
    return pl.pallas_call(
        functools.partial(cross_kernel, widths, base is not None, has_turn),
        grid_spec=pltpu.PrefetchScalarGridSpec(
            num_scalar_prefetch=2,
            grid=(columns // TILE,),
            in_specs=in_specs,
            out_specs=out_specs,
            scratch_shapes=[pltpu.VMEM((rows, sum(widths)), jnp.bfloat16)] * 2,
        ),
        out_shape=[jax.ShapeDtypeStruct(shape, jnp.float32) for shape in shapes],
        compiler_params=pltpu.CompilerParams(vmem_limit_bytes=VMEM_LIMIT),
        cost_estimate=pl.CostEstimate(flops=1000, bytes_accessed=1000, transcendentals=0),
    )(*operands)


def in_order(is_first, mine, theirs):
    return jnp.where(is_first, mine, theirs), jnp.where(is_first, theirs, mine)


def inner_kernel(pieces, widths, spots, core, mine, theirs, *refs):
    rights, base = refs[:len(widths)], refs[len(widths)]
    out, left = refs[-2:]

    @pl.when(pl.program_id(0) == 0)
    def _():
        is_first = core[0] == 0
        at = 0
        for j, halves in enumerate(pieces):
            both = in_order(is_first, mine[spots[j]], theirs[spots[j]])
            for half in halves:
                left[:LANES, at:at + LANES], left[LANES:, at:at + LANES] = split(both[half].T)
                at += LANES

    out[...] = base[...] - stacked_pass(left, rights, widths)


def inner_sum(base, mine, theirs, spots, core, pieces, rights):
    rows, columns = base.shape
    widths = tuple(array.shape[0] for array in rights)
    whole = pl.BlockSpec(mine.shape, lambda n, spots, core: (0, 0, 0))
    tile = pl.BlockSpec((rows, TILE), lambda n, spots, core: (0, n))
    return pl.pallas_call(
        functools.partial(inner_kernel, pieces, widths),
        grid_spec=pltpu.PrefetchScalarGridSpec(
            num_scalar_prefetch=2,
            grid=(columns // TILE,),
            in_specs=[whole, whole]
            + [pl.BlockSpec((width, TILE), lambda n, spots, core: (0, n)) for width in widths]
            + [tile],
            out_specs=tile,
            scratch_shapes=[pltpu.VMEM((2 * rows, sum(widths)), jnp.bfloat16)],
        ),
        out_shape=jax.ShapeDtypeStruct(base.shape, jnp.float32),
        compiler_params=pltpu.CompilerParams(vmem_limit_bytes=VMEM_LIMIT),
        cost_estimate=pl.CostEstimate(flops=1000, bytes_accessed=1000, transcendentals=0),
    )(spots, core, mine, theirs, *rights, base)


def pick_kernel(spots, core, root, mine, theirs, high, low):
    for j in range(spots.shape[0]):
        spot, at = spots[j], slice(j * BLK, (j + 1) * BLK)

        @pl.when(spot < CHIPS)
        def _():
            high[:, at], low[:, at] = split(root[:, pl.ds(pl.multiple_of(spot * BLK, BLK), BLK)])

        @pl.when(spot >= CHIPS)
        def _():
            block = spot - CHIPS
            columns = pl.ds(pl.multiple_of((block % PER_CORE) * BLK, BLK), BLK)
            ours = block // PER_CORE == core[0]
            high[:, at], low[:, at] = split(jnp.where(ours, mine[:, columns], theirs[:, columns]))


def pick(spots, core, root, cross, cross_theirs):
    shape = jax.ShapeDtypeStruct((root.shape[0], spots.shape[0] * BLK), jnp.bfloat16)
    space = pl.BlockSpec(memory_space=pltpu.VMEM)
    scalars = [pl.BlockSpec(memory_space=pltpu.SMEM)] * 2
    return pl.pallas_call(
        pick_kernel,
        in_specs=scalars + [space] * 3,
        out_specs=[space] * 2,
        out_shape=[shape] * 2,
        compiler_params=pltpu.CompilerParams(vmem_limit_bytes=VMEM_LIMIT),
        cost_estimate=pl.CostEstimate(flops=0, bytes_accessed=20 * root.size, transcendentals=0),
    )(spots, core, root, cross, cross_theirs)


def halves_of(out, core, keep, give):
    rows = keep.shape[1]
    for ref, half in ((keep, core), (give, 1 - core)):
        for k in range(ref.shape[0]):
            ref[k] = out[pl.ds(pl.multiple_of(half * rows, rows), rows), k * LANES:(k + 1) * LANES]


def column_kernel(spots, core, top_high, top_low, *refs):
    step = pl.program_id(0)
    lefts, (lower, out_top, out_low, keep, give, high, low) = refs[:4 * GROUP], refs[4 * GROUP:]
    turns, turn_others, inners, inner_others = [lefts[kind * GROUP:(kind + 1) * GROUP] for kind in range(4)]
    top = out_top.shape[0]
    high[:top, :], low[:top, :] = top_high[...], top_low[...]

    for q in range(GROUP):
        spot, at = spots[step * GROUP + q], q * BLK

        def store(columns, value):
            high[top:, columns], low[top:, columns] = split(value)

        @pl.when(spot < CHIPS)
        def _():
            for half, value in enumerate(in_order(core[0] == 0, turns[q][0], turn_others[q][0])):
                store(slice(at + half * LANES, at + (half + 1) * LANES), value.T)

        @pl.when(spot >= CHIPS)
        def _():
            ours = (spot - CHIPS) // PER_CORE == core[0]
            store(slice(at, at + BLK), jnp.where(ours, inners[q][...], inner_others[q][...]))

    for n in range(0, lower.shape[1], TILE):
        columns = slice(n, n + TILE)
        total = three_pass(high, low, [lower.at[:, columns]], [lower.shape[0]])

        @pl.when(step == 0)
        def _():
            out_top[:, columns], out_low[:, columns] = -total[:top], -total[top:]

        @pl.when(step > 0)
        def _():
            out_top[:, columns] -= total[:top]
            out_low[:, columns] -= total[top:]

    @pl.when(step == pl.num_programs(0) - 1)
    def _():
        halves_of(out_top, core[0], keep.at[:, :LANES], give.at[:, :LANES])
        halves_of(out_low, core[0], keep.at[:, LANES:], give.at[:, LANES:])


def column_sum(spots, core, picked, turned, turned_theirs, inner, inner_theirs, lower):
    top, low, columns = picked[0].shape[0], inner.shape[0], lower.shape[1]

    def listed(shape, place):
        return [
            pl.BlockSpec(shape, functools.partial(lambda q, k, spots, core: place(spots[k * GROUP + q]), q))
            for q in range(GROUP)
        ]

    def block(spot):
        return jnp.maximum(spot - CHIPS, 0) % PER_CORE

    in_specs = [pl.BlockSpec((top, GROUP * BLK), lambda k, spots, core: (0, k))] * 2
    in_specs += 2 * listed((1, LANES, LANES), lambda spot: (jnp.minimum(spot, CHIPS - 1), 0, 0))
    in_specs += 2 * listed((low, BLK), lambda spot: (0, block(spot)))
    in_specs.append(pl.BlockSpec((GROUP * BLK, columns), lambda k, spots, core: (k, 0)))
    operands = [x for x in (turned, turned_theirs, inner, inner_theirs) for _ in range(GROUP)]
    shapes = [(top, columns), (low, columns)] + [(columns // LANES, (top + low) // 2, LANES)] * 2
    return pl.pallas_call(
        column_kernel,
        grid_spec=pltpu.PrefetchScalarGridSpec(
            num_scalar_prefetch=2,
            grid=(spots.shape[0] // GROUP,),
            in_specs=in_specs,
            out_specs=[
                pl.BlockSpec(shape, functools.partial(lambda size, k, spots, core: (0,) * size, len(shape)))
                for shape in shapes
            ],
            scratch_shapes=[pltpu.VMEM((top + low, GROUP * BLK), jnp.bfloat16)] * 2,
        ),
        out_shape=[jax.ShapeDtypeStruct(shape, jnp.float32) for shape in shapes],
        compiler_params=pltpu.CompilerParams(vmem_limit_bytes=VMEM_LIMIT),
        cost_estimate=pl.CostEstimate(flops=1000, bytes_accessed=1000, transcendentals=0),
    )(spots, core, *picked, *operands, lower)


def last_kernel(spots, core, mine, theirs, lower, base, out, high, low):
    @pl.when(pl.program_id(0) == 0)
    def _():
        is_first = core[0] == 0
        for j in range(spots.shape[0]):
            spot = spots[j]

            def store(parts):
                for half, value in enumerate(parts):
                    at = slice(j * BLK + half * LANES, j * BLK + (half + 1) * LANES)
                    high[:, at], low[:, at] = split(value.T)

            @pl.when(spot < CHIPS)
            def _():
                store(in_order(is_first, mine[spot, :LANES, :], theirs[spot, :LANES, :]))

            @pl.when(spot >= CHIPS)
            def _():
                chips = (2 * (spot - CHIPS), 2 * (spot - CHIPS) + 1)
                store([jnp.concatenate(in_order(is_first, mine[c, LANES:, :], theirs[c, LANES:, :])) for c in chips])

    out[...] = base[...] - three_pass(high, low, [lower], [lower.shape[0]])


def last_sum(base, mine, theirs, spots, core, lower):
    rows, columns = base.shape
    whole = pl.BlockSpec(mine.shape, lambda n, spots, core: (0, 0, 0))
    tile = pl.BlockSpec((rows, TILE), lambda n, spots, core: (0, n))
    return pl.pallas_call(
        last_kernel,
        grid_spec=pltpu.PrefetchScalarGridSpec(
            num_scalar_prefetch=2,
            grid=(columns // TILE,),
            in_specs=[whole, whole, pl.BlockSpec((lower.shape[0], TILE), lambda n, spots, core: (0, n)), tile],
            out_specs=tile,
            scratch_shapes=[pltpu.VMEM((rows, lower.shape[0]), jnp.bfloat16)] * 2,
        ),
        out_shape=jax.ShapeDtypeStruct(base.shape, jnp.float32),
        compiler_params=pltpu.CompilerParams(vmem_limit_bytes=VMEM_LIMIT),
        cost_estimate=pl.CostEstimate(flops=1000, bytes_accessed=1000, transcendentals=0),
    )(spots, core, mine, theirs, lower, base)


def after(value, *others):
    return lax.optimization_barrier((value,) + others)[0]


def pull(value, way):
    pairs = []
    for target in range(CHIPS):
        y, x = divmod(target, SIDE)
        pairs.append((((y + way[0]) % SIDE) * SIDE + (x + way[1]) % SIDE, target))
    return lax.ppermute(value, "row", pairs)


def other_core(value):
    return lax.ppermute(value, "col", [(0, 1), (1, 0)])


def turn(core, keep, give):
    sent = jnp.concatenate(in_order(core == 0, keep, other_core(give)), axis=0)
    return lax.all_to_all(sent, "row", split_axis=0, concat_axis=0, tiled=True)


def first_round(own):
    return [pull(own, way) for way in (EAST, WEST, SOUTH, NORTH)]


def second_round(near, *gates):
    e, w, s, n = near
    es = pull(after(s, e, *gates), EAST)
    wn = pull(after(n, w, *gates), WEST)
    sw = pull(after(w, s, *gates), SOUTH)
    ne = pull(after(e, n, *gates), NORTH)
    return es, wn, sw, ne


def third_round(diagonal, *gates):
    es, wn, sw, ne = diagonal
    ees = pull(after(es, *gates), EAST)
    wwn = pull(after(wn, *gates), WEST)
    sse = pull(after(es, sw, *gates), SOUTH)
    nnw = pull(after(wn, ne, *gates), NORTH)
    return ees, wwn, sse, nnw


def fourth_round(near, third, *gates):
    e, w, s, n = near
    ees, wwn, sse, nnw = third
    half = e.shape[0] // 2
    first = pull(after(nnw[:half], wwn, *gates), WEST)
    second = pull(after(wwn[half:], nnw, *gates), NORTH)
    return pull(after(e, ees, *gates), EAST), pull(after(s, sse, *gates), SOUTH), first, second


PLACES = [
    [(0, 0), EAST, WEST, SOUTH, NORTH, (1, 1), (3, 3), (1, 3), (3, 1)],
    [(1, 2), (3, 2), (2, 1), (2, 3)],
    [(0, 2), (2, 0), (2, 2), (2, 2)],
]
WHOLE = (0, 1)
HALVES = [[WHOLE] * 9, [WHOLE] * 4, [WHOLE, WHOLE, (0,), (1,)]]


def body(root_inverse, panel_one, diag_one, panel_two, diag_two, structure):
    place = lax.axis_index("row")
    core = lax.axis_index("col").astype(jnp.int32)
    core_vector = core[None]
    blocks = structure[0, 0]
    own_upper, own_lower = panel_one[0], panel_two[0, 0]

    def chips(places):
        down = jnp.array([spot[0] for spot in places], jnp.int32)
        right = jnp.array([spot[1] for spot in places], jnp.int32)
        return ((place // SIDE + down) % SIDE) * SIDE + (place % SIDE + right) % SIDE

    halves = sum(HALVES, [])
    every_spots = chips(sum(PLACES, []))
    late_spots = chips(PLACES[2]) * jnp.array([1, 1, 2, 2], jnp.int32) + jnp.array([0, 0, 0, 1], jnp.int32)

    root_rows = lax.all_gather(root_inverse, ("leaf", "col"), axis=1, tiled=True)

    near = first_round(own_upper)
    diagonal = second_round(near)
    third = third_round(diagonal)
    lower = lax.all_gather(after(own_lower, *near), "row", axis=0, tiled=True)
    early = [own_upper, *near, *diagonal]
    cross, = cross_sum(None, root_rows, every_spots[:9], core_vector, early)
    fourth = fourth_round(near, third)
    cross, = cross_sum(cross, root_rows, every_spots[9:13], core_vector, third)
    cross, keep, give = cross_sum(cross, root_rows, late_spots, core_vector, fourth, True)
    turned = turn(core, keep, give)
    picked = pick(blocks, core_vector, root_rows, cross, other_core(cross))
    turned = after(turned, *picked)
    turned_theirs = other_core(turned)
    upper = [*early, *third, *fourth]
    inner = inner_sum(diag_one[0], turned, turned_theirs, every_spots, core_vector, sum(HALVES, []), upper)

    top, low, keep, give = column_sum(
        blocks, core_vector, picked, turned, turned_theirs, inner, other_core(inner), lower
    )
    turned = turn(core, keep, give)
    inner_low = last_sum(diag_two[0, 0], turned, other_core(turned), blocks, core_vector, lower)
    return cross[None], inner[None], top[None, None], low[None, None], inner_low[None, None]


def solution(mesh):
    in_specs = (
        P("row", ("leaf", "col")),
        P("leaf", "row", "col"),
        P("leaf", "row", "col"),
        P("leaf", None, "row", "col"),
        P("leaf", None, "row", "col"),
        P("leaf", None, None),
    )
    out_specs = (
        P("leaf", "row", "col"),
        P("leaf", "row", "col"),
        P("leaf", None, "row", "col"),
        P("leaf", None, "row", "col"),
        P("leaf", None, "row", "col"),
    )
    return jax.shard_map(body, mesh=mesh, in_specs=in_specs, out_specs=out_specs, check_vma=False)
```

```python
import functools

import jax
import jax.numpy as jnp
from jax import lax
from jax.experimental import pallas as pl
from jax.experimental.pallas import tpu as pltpu
from jax.sharding import PartitionSpec as P

BLK = 256
LANES = 128
SIDE = 4
CHIPS = SIDE * SIDE
TILE = 512
GROUP = 4
PER_CORE = 4
VMEM_LIMIT = 60 * 1024 * 1024
EAST, WEST, SOUTH, NORTH = (0, 1), (0, 3), (1, 0), (3, 0)


def split(value):
    high = value.astype(jnp.bfloat16)
    return high, (value - high.astype(jnp.float32)).astype(jnp.bfloat16)


def mxu(left, right):
    return jnp.dot(left, right, preferred_element_type=jnp.float32)


def three_pass(left_high, left_low, rights, widths):
    total, at = None, 0
    for ref, width in zip(rights, widths):
        for start in range(0, width, BLK):
            size = min(BLK, width - start)
            high, low = split(ref[start:start + size, :])
            ours = left_high[:, at:at + size]
            term = mxu(ours, high) + mxu(ours, low) + mxu(left_low[:, at:at + size], high)
            total = term if total is None else total + term
            at += size
    return total


def cross_kernel(widths, has_base, has_turn, spots, core, *refs):
    count = len(widths)
    lefts, rights, rest = refs[:count], refs[count:2 * count], refs[2 * count:]
    base = rest[0] if has_base else None
    out, *turning, left_high, left_low = rest[1:] if has_base else rest

    @pl.when(pl.program_id(0) == 0)
    def _():
        at = 0
        for ref, width in zip(lefts, widths):
            left_high[:, at:at + width], left_low[:, at:at + width] = split(ref[...])
            at += width

    total = three_pass(left_high, left_low, rights, widths)
    out[...] = base[...] - total if has_base else -total
    if has_turn:
        halves_of(out, core[0], *turning)


def cross_sum(base, left, spots, core, rights, has_turn=False):
    rows, columns = left.shape[0], rights[0].shape[1]
    widths = tuple(array.shape[0] for array in rights)
    tile = pl.BlockSpec((rows, TILE), lambda n, spots, core: (0, n))
    in_specs = [
        pl.BlockSpec((rows, width), functools.partial(lambda j, n, spots, core: (0, spots[j]), j))
        for j, width in enumerate(widths)
    ] + [pl.BlockSpec((width, TILE), lambda n, spots, core: (0, n)) for width in widths]
    operands = [spots, core] + [left] * len(rights) + list(rights)
    if base is not None:
        in_specs.append(tile)
        operands.append(base)
    out_specs, shapes = [tile], [(rows, columns)]
    if has_turn:
        out_specs += [pl.BlockSpec((TILE // LANES, rows // 2, LANES), lambda n, spots, core: (n, 0, 0))] * 2
        shapes += [(columns // LANES, rows // 2, LANES)] * 2
    return pl.pallas_call(
        functools.partial(cross_kernel, widths, base is not None, has_turn),
        grid_spec=pltpu.PrefetchScalarGridSpec(
            num_scalar_prefetch=2,
            grid=(columns // TILE,),
            in_specs=in_specs,
            out_specs=out_specs,
            scratch_shapes=[pltpu.VMEM((rows, sum(widths)), jnp.bfloat16)] * 2,
        ),
        out_shape=[jax.ShapeDtypeStruct(shape, jnp.float32) for shape in shapes],
        compiler_params=pltpu.CompilerParams(vmem_limit_bytes=VMEM_LIMIT),
        cost_estimate=pl.CostEstimate(flops=1000, bytes_accessed=1000, transcendentals=0),
    )(*operands)


def in_order(is_first, mine, theirs):
    return jnp.where(is_first, mine, theirs), jnp.where(is_first, theirs, mine)


def inner_kernel(pieces, spots, core, mine, theirs, *refs):
    rights, (base, out, turned_high, turned_low) = refs[:len(pieces)], refs[len(pieces):]

    @pl.when(pl.program_id(0) == 0)
    def _():
        for chip in range(CHIPS):
            for half, value in enumerate(in_order(core[0] == 0, mine[chip], theirs[chip])):
                at = slice(chip * BLK + half * LANES, chip * BLK + (half + 1) * LANES)
                turned_high[:, at], turned_low[:, at] = split(value.T)

    total = base[...]
    for j, (ref, halves) in enumerate(zip(rights, pieces)):
        high, low = split(ref[...])
        columns = pl.ds(pl.multiple_of(spots[j] * BLK + halves[0] * LANES, LANES), ref.shape[0])
        ours = turned_high[:, columns]
        total -= mxu(ours, high) + mxu(ours, low) + mxu(turned_low[:, columns], high)
    out[...] = total


def inner_sum(base, mine, theirs, spots, core, pieces, rights):
    rows, columns = base.shape
    depth = 2 * mine.shape[0] * mine.shape[1]
    whole = pl.BlockSpec(mine.shape, lambda n, spots, core: (0, 0, 0))
    tile = pl.BlockSpec((rows, TILE), lambda n, spots, core: (0, n))
    part = pl.BlockSpec((rows, depth), lambda n, spots, core: (0, 0))
    out, *turned = pl.pallas_call(
        functools.partial(inner_kernel, pieces),
        grid_spec=pltpu.PrefetchScalarGridSpec(
            num_scalar_prefetch=2,
            grid=(columns // TILE,),
            in_specs=[whole, whole]
            + [pl.BlockSpec((array.shape[0], TILE), lambda n, spots, core: (0, n)) for array in rights]
            + [tile],
            out_specs=[tile, part, part],
        ),
        out_shape=[jax.ShapeDtypeStruct(base.shape, jnp.float32)]
        + [jax.ShapeDtypeStruct((rows, depth), jnp.bfloat16)] * 2,
        compiler_params=pltpu.CompilerParams(vmem_limit_bytes=VMEM_LIMIT),
        cost_estimate=pl.CostEstimate(flops=1000, bytes_accessed=1000, transcendentals=0),
    )(spots, core, mine, theirs, *rights, base)
    return out, turned


def pick_kernel(spots, core, root, mine, theirs, high, low):
    for j in range(spots.shape[0]):
        spot, at = spots[j], slice(j * BLK, (j + 1) * BLK)

        @pl.when(spot < CHIPS)
        def _():
            high[:, at], low[:, at] = split(root[:, pl.ds(pl.multiple_of(spot * BLK, BLK), BLK)])

        @pl.when(spot >= CHIPS)
        def _():
            block = spot - CHIPS
            columns = pl.ds(pl.multiple_of((block % PER_CORE) * BLK, BLK), BLK)
            ours = block // PER_CORE == core[0]
            high[:, at], low[:, at] = split(jnp.where(ours, mine[:, columns], theirs[:, columns]))


def pick(spots, core, root, cross, cross_theirs):
    shape = jax.ShapeDtypeStruct((root.shape[0], spots.shape[0] * BLK), jnp.bfloat16)
    space = pl.BlockSpec(memory_space=pltpu.VMEM)
    scalars = [pl.BlockSpec(memory_space=pltpu.SMEM)] * 2
    return pl.pallas_call(
        pick_kernel,
        in_specs=scalars + [space] * 3,
        out_specs=[space] * 2,
        out_shape=[shape] * 2,
        compiler_params=pltpu.CompilerParams(vmem_limit_bytes=VMEM_LIMIT),
        cost_estimate=pl.CostEstimate(flops=0, bytes_accessed=20 * root.size, transcendentals=0),
    )(spots, core, root, cross, cross_theirs)


def halves_of(out, core, keep, give):
    rows = keep.shape[1]
    for ref, half in ((keep, core), (give, 1 - core)):
        for k in range(ref.shape[0]):
            ref[k] = out[pl.ds(pl.multiple_of(half * rows, rows), rows), k * LANES:(k + 1) * LANES]


def column_kernel(spots, core, top_high, top_low, *refs):
    step = pl.program_id(0)
    lefts, (lower, out_top, out_low, keep, give, high, low) = refs[:4 * GROUP], refs[4 * GROUP:]
    turned_high, turned_low, inners, inner_others = [lefts[kind * GROUP:(kind + 1) * GROUP] for kind in range(4)]
    top = out_top.shape[0]
    high[:top, :], low[:top, :] = top_high[...], top_low[...]

    for q in range(GROUP):
        spot, at = spots[step * GROUP + q], q * BLK

        @pl.when(spot < CHIPS)
        def _():
            columns = slice(at, at + BLK)
            high[top:, columns], low[top:, columns] = turned_high[q][...], turned_low[q][...]

        @pl.when(spot >= CHIPS)
        def _():
            ours = (spot - CHIPS) // PER_CORE == core[0]
            columns = slice(at, at + BLK)
            high[top:, columns], low[top:, columns] = split(jnp.where(ours, inners[q][...], inner_others[q][...]))

    for n in range(0, lower.shape[1], TILE):
        columns = slice(n, n + TILE)
        total = three_pass(high, low, [lower.at[:, columns]], [lower.shape[0]])

        @pl.when(step == 0)
        def _():
            out_top[:, columns], out_low[:, columns] = -total[:top], -total[top:]

        @pl.when(step > 0)
        def _():
            out_top[:, columns] -= total[:top]
            out_low[:, columns] -= total[top:]

    @pl.when(step == pl.num_programs(0) - 1)
    def _():
        halves_of(out_top, core[0], keep.at[:, :LANES], give.at[:, :LANES])
        halves_of(out_low, core[0], keep.at[:, LANES:], give.at[:, LANES:])


def column_sum(spots, core, picked, turned, inner, inner_theirs, lower):
    top, low, columns = picked[0].shape[0], inner.shape[0], lower.shape[1]

    def listed(shape, place):
        return [
            pl.BlockSpec(shape, functools.partial(lambda q, k, spots, core: place(spots[k * GROUP + q]), q))
            for q in range(GROUP)
        ]

    def block(spot):
        return jnp.maximum(spot - CHIPS, 0) % PER_CORE

    in_specs = [pl.BlockSpec((top, GROUP * BLK), lambda k, spots, core: (0, k))] * 2
    in_specs += 2 * listed((low, BLK), lambda spot: (0, jnp.minimum(spot, CHIPS - 1)))
    in_specs += 2 * listed((low, BLK), lambda spot: (0, block(spot)))
    in_specs.append(pl.BlockSpec((GROUP * BLK, columns), lambda k, spots, core: (k, 0)))
    operands = [x for x in (*turned, inner, inner_theirs) for _ in range(GROUP)]
    shapes = [(top, columns), (low, columns)] + [(columns // LANES, (top + low) // 2, LANES)] * 2
    return pl.pallas_call(
        column_kernel,
        grid_spec=pltpu.PrefetchScalarGridSpec(
            num_scalar_prefetch=2,
            grid=(spots.shape[0] // GROUP,),
            in_specs=in_specs,
            out_specs=[
                pl.BlockSpec(shape, functools.partial(lambda size, k, spots, core: (0,) * size, len(shape)))
                for shape in shapes
            ],
            scratch_shapes=[pltpu.VMEM((top + low, GROUP * BLK), jnp.bfloat16)] * 2,
        ),
        out_shape=[jax.ShapeDtypeStruct(shape, jnp.float32) for shape in shapes],
        compiler_params=pltpu.CompilerParams(vmem_limit_bytes=VMEM_LIMIT),
        cost_estimate=pl.CostEstimate(flops=1000, bytes_accessed=1000, transcendentals=0),
    )(spots, core, *picked, *operands, lower)


def last_kernel(spots, core, mine, theirs, lower, base, out, high, low):
    @pl.when(pl.program_id(0) == 0)
    def _():
        is_first = core[0] == 0
        for j in range(spots.shape[0]):
            spot = spots[j]
            chip, first_low = jnp.minimum(spot, CHIPS - 1), jnp.maximum(2 * (spot - CHIPS), 0)
            parts = in_order(is_first, mine[chip, :LANES, :], theirs[chip, :LANES, :])
            for half, value in enumerate(parts):
                c = first_low + half
                lower_rows = jnp.concatenate(in_order(is_first, mine[c, LANES:, :], theirs[c, LANES:, :]))
                at = slice(j * BLK + half * LANES, j * BLK + (half + 1) * LANES)
                high[:, at], low[:, at] = split(jnp.where(spot < CHIPS, value, lower_rows).T)

    out[...] = base[...] - three_pass(high, low, [lower], [lower.shape[0]])


def last_sum(base, mine, theirs, spots, core, lower):
    rows, columns = base.shape
    whole = pl.BlockSpec(mine.shape, lambda n, spots, core: (0, 0, 0))
    tile = pl.BlockSpec((rows, TILE), lambda n, spots, core: (0, n))
    return pl.pallas_call(
        last_kernel,
        grid_spec=pltpu.PrefetchScalarGridSpec(
            num_scalar_prefetch=2,
            grid=(columns // TILE,),
            in_specs=[whole, whole, pl.BlockSpec((lower.shape[0], TILE), lambda n, spots, core: (0, n)), tile],
            out_specs=tile,
            scratch_shapes=[pltpu.VMEM((rows, lower.shape[0]), jnp.bfloat16)] * 2,
        ),
        out_shape=jax.ShapeDtypeStruct(base.shape, jnp.float32),
        compiler_params=pltpu.CompilerParams(vmem_limit_bytes=VMEM_LIMIT),
        cost_estimate=pl.CostEstimate(flops=1000, bytes_accessed=1000, transcendentals=0),
    )(spots, core, mine, theirs, lower, base)


def after(value, *others):
    return lax.optimization_barrier((value,) + others)[0]


def pull(value, way):
    pairs = []
    for target in range(CHIPS):
        y, x = divmod(target, SIDE)
        pairs.append((((y + way[0]) % SIDE) * SIDE + (x + way[1]) % SIDE, target))
    return lax.ppermute(value, "row", pairs)


def other_core(value):
    return lax.ppermute(value, "col", [(0, 1), (1, 0)])


def turn(core, keep, give):
    sent = jnp.concatenate(in_order(core == 0, keep, other_core(give)), axis=0)
    return lax.all_to_all(sent, "row", split_axis=0, concat_axis=0, tiled=True)


def first_round(own):
    return [pull(own, way) for way in (EAST, WEST, SOUTH, NORTH)]


def second_round(near, *gates):
    e, w, s, n = near
    es = pull(after(s, e, *gates), EAST)
    wn = pull(after(n, w, *gates), WEST)
    sw = pull(after(w, s, *gates), SOUTH)
    ne = pull(after(e, n, *gates), NORTH)
    return es, wn, sw, ne


def third_round(diagonal, *gates):
    es, wn, sw, ne = diagonal
    ees = pull(after(es, *gates), EAST)
    wwn = pull(after(wn, *gates), WEST)
    sse = pull(after(es, sw, *gates), SOUTH)
    nnw = pull(after(wn, ne, *gates), NORTH)
    return ees, wwn, sse, nnw


def fourth_round(near, third, *gates):
    e, w, s, n = near
    ees, wwn, sse, nnw = third
    half = e.shape[0] // 2
    first = pull(after(nnw[:half], wwn, *gates), WEST)
    second = pull(after(wwn[half:], nnw, *gates), NORTH)
    return pull(after(e, ees, *gates), EAST), pull(after(s, sse, *gates), SOUTH), first, second


PLACES = [
    [(0, 0), EAST, WEST, SOUTH, NORTH, (1, 1), (3, 3), (1, 3), (3, 1)],
    [(1, 2), (3, 2), (2, 1), (2, 3)],
    [(0, 2), (2, 0), (2, 2), (2, 2)],
]
WHOLE = (0, 1)
HALVES = [[WHOLE] * 9, [WHOLE] * 4, [WHOLE, WHOLE, (0,), (1,)]]


def body(root_inverse, panel_one, diag_one, panel_two, diag_two, structure):
    place = lax.axis_index("row")
    core = lax.axis_index("col").astype(jnp.int32)
    core_vector = core[None]
    blocks = structure[0, 0]
    own_upper, own_lower = panel_one[0], panel_two[0, 0]

    def chips(places):
        down = jnp.array([spot[0] for spot in places], jnp.int32)
        right = jnp.array([spot[1] for spot in places], jnp.int32)
        return ((place // SIDE + down) % SIDE) * SIDE + (place % SIDE + right) % SIDE

    halves = sum(HALVES, [])
    every_spots = chips(sum(PLACES, []))
    late_spots = chips(PLACES[2]) * jnp.array([1, 1, 2, 2], jnp.int32) + jnp.array([0, 0, 0, 1], jnp.int32)

    root_rows = lax.all_gather(root_inverse, ("leaf", "col"), axis=1, tiled=True)

    near = first_round(own_upper)
    diagonal = second_round(near)
    third = third_round(diagonal)
    lower = lax.all_gather(after(own_lower, *near), "row", axis=0, tiled=True)
    early = [own_upper, *near, *diagonal]
    cross, = cross_sum(None, root_rows, every_spots[:9], core_vector, early)
    fourth = fourth_round(near, third)
    cross, = cross_sum(cross, root_rows, every_spots[9:13], core_vector, third)
    cross, keep, give = cross_sum(cross, root_rows, late_spots, core_vector, fourth, True)
    turned = turn(core, keep, give)
    picked = pick(blocks, core_vector, root_rows, cross, other_core(cross))
    turned = after(turned, *picked)
    turned_theirs = other_core(turned)
    upper = [*early, *third, *fourth]
    inner, turned_parts = inner_sum(diag_one[0], turned, turned_theirs, every_spots, core_vector, sum(HALVES, []), upper)

    top, low, keep, give = column_sum(
        blocks, core_vector, picked, turned_parts, inner, other_core(inner), lower
    )
    turned = turn(core, keep, give)
    inner_low = last_sum(diag_two[0, 0], turned, other_core(turned), blocks, core_vector, lower)
    return cross[None], inner[None], top[None, None], low[None, None], inner_low[None, None]


def solution(mesh):
    in_specs = (
        P("row", ("leaf", "col")),
        P("leaf", "row", "col"),
        P("leaf", "row", "col"),
        P("leaf", None, "row", "col"),
        P("leaf", None, "row", "col"),
        P("leaf", None, None),
    )
    out_specs = (
        P("leaf", "row", "col"),
        P("leaf", "row", "col"),
        P("leaf", None, "row", "col"),
        P("leaf", None, "row", "col"),
        P("leaf", None, "row", "col"),
    )
    return jax.shard_map(body, mesh=mesh, in_specs=in_specs, out_specs=out_specs, check_vma=False)
```

```python
import functools

import jax
import jax.numpy as jnp
from jax import lax
from jax.experimental import pallas as pl
from jax.experimental.pallas import tpu as pltpu
from jax.sharding import PartitionSpec as P

BLK = 256
LANES = 128
SIDE = 4
CHIPS = SIDE * SIDE
TILE = 512
GROUP = 4
PER_CORE = 4
VMEM_LIMIT = 60 * 1024 * 1024
EAST, WEST, SOUTH, NORTH = (0, 1), (0, 3), (1, 0), (3, 0)


def split(value):
    high = value.astype(jnp.bfloat16)
    return high, (value - high.astype(jnp.float32)).astype(jnp.bfloat16)


def mxu(left, right):
    return jnp.dot(left, right, preferred_element_type=jnp.float32)


def three_pass(left_high, left_low, rights, widths):
    total, at = None, 0
    for ref, width in zip(rights, widths):
        for start in range(0, width, BLK):
            size = min(BLK, width - start)
            high, low = split(ref[start:start + size, :])
            ours = left_high[:, at:at + size]
            term = mxu(ours, high) + mxu(ours, low) + mxu(left_low[:, at:at + size], high)
            total = term if total is None else total + term
            at += size
    return total


def cross_kernel(widths, has_base, has_turn, spots, core, *refs):
    count = len(widths)
    lefts, rights, rest = refs[:count], refs[count:2 * count], refs[2 * count:]
    base = rest[0] if has_base else None
    out, *turning, left_high, left_low = rest[1:] if has_base else rest

    @pl.when(pl.program_id(0) == 0)
    def _():
        at = 0
        for ref, width in zip(lefts, widths):
            left_high[:, at:at + width], left_low[:, at:at + width] = split(ref[...])
            at += width

    total = three_pass(left_high, left_low, rights, widths)
    out[...] = base[...] - total if has_base else -total
    if has_turn:
        halves_of(out, core[0], *turning)


def cross_sum(base, left, spots, core, rights, has_turn=False):
    rows, columns = left.shape[0], rights[0].shape[1]
    widths = tuple(array.shape[0] for array in rights)
    tile = pl.BlockSpec((rows, TILE), lambda n, spots, core: (0, n))
    in_specs = [
        pl.BlockSpec((rows, width), functools.partial(lambda j, n, spots, core: (0, spots[j]), j))
        for j, width in enumerate(widths)
    ] + [pl.BlockSpec((width, TILE), lambda n, spots, core: (0, n)) for width in widths]
    operands = [spots, core] + [left] * len(rights) + list(rights)
    if base is not None:
        in_specs.append(tile)
        operands.append(base)
    out_specs, shapes = [tile], [(rows, columns)]
    if has_turn:
        out_specs += [pl.BlockSpec((TILE // LANES, rows // 2, LANES), lambda n, spots, core: (n, 0, 0))] * 2
        shapes += [(columns // LANES, rows // 2, LANES)] * 2
    return pl.pallas_call(
        functools.partial(cross_kernel, widths, base is not None, has_turn),
        grid_spec=pltpu.PrefetchScalarGridSpec(
            num_scalar_prefetch=2,
            grid=(columns // TILE,),
            in_specs=in_specs,
            out_specs=out_specs,
            scratch_shapes=[pltpu.VMEM((rows, sum(widths)), jnp.bfloat16)] * 2,
        ),
        out_shape=[jax.ShapeDtypeStruct(shape, jnp.float32) for shape in shapes],
        compiler_params=pltpu.CompilerParams(vmem_limit_bytes=VMEM_LIMIT),
        cost_estimate=pl.CostEstimate(flops=1000, bytes_accessed=1000, transcendentals=0),
    )(*operands)


def in_order(is_first, mine, theirs):
    return jnp.where(is_first, mine, theirs), jnp.where(is_first, theirs, mine)


def inner_kernel(pieces, spots, core, mine, theirs, *refs):
    rights, (base, out, turned_high, turned_low) = refs[:len(pieces)], refs[len(pieces):]

    @pl.when(pl.program_id(0) == 0)
    def _():
        for chip in range(CHIPS):
            for half, value in enumerate(in_order(core[0] == 0, mine[chip], theirs[chip])):
                at = slice(chip * BLK + half * LANES, chip * BLK + (half + 1) * LANES)
                turned_high[:, at], turned_low[:, at] = split(value.T)

    total = base[...]
    for j, (ref, halves) in enumerate(zip(rights, pieces)):
        high, low = split(ref[...])
        columns = pl.ds(pl.multiple_of(spots[j] * BLK + halves[0] * LANES, LANES), ref.shape[0])
        ours = turned_high[:, columns]
        total -= mxu(ours, high) + mxu(ours, low) + mxu(turned_low[:, columns], high)
    out[...] = total


def inner_sum(base, mine, theirs, spots, core, pieces, rights):
    rows, columns = base.shape
    depth = 2 * mine.shape[0] * mine.shape[1]
    whole = pl.BlockSpec(mine.shape, lambda n, spots, core: (0, 0, 0))
    tile = pl.BlockSpec((rows, TILE), lambda n, spots, core: (0, n))
    part = pl.BlockSpec((rows, depth), lambda n, spots, core: (0, 0))
    out, *turned = pl.pallas_call(
        functools.partial(inner_kernel, pieces),
        grid_spec=pltpu.PrefetchScalarGridSpec(
            num_scalar_prefetch=2,
            grid=(columns // TILE,),
            in_specs=[whole, whole]
            + [pl.BlockSpec((array.shape[0], TILE), lambda n, spots, core: (0, n)) for array in rights]
            + [tile],
            out_specs=[tile, part, part],
        ),
        out_shape=[jax.ShapeDtypeStruct(base.shape, jnp.float32)]
        + [jax.ShapeDtypeStruct((rows, depth), jnp.bfloat16)] * 2,
        compiler_params=pltpu.CompilerParams(vmem_limit_bytes=VMEM_LIMIT),
        cost_estimate=pl.CostEstimate(flops=1000, bytes_accessed=1000, transcendentals=0),
    )(spots, core, mine, theirs, *rights, base)
    return out, turned


def pick_kernel(spots, core, root, mine, theirs, high, low):
    for j in range(spots.shape[0]):
        spot, at = spots[j], slice(j * BLK, (j + 1) * BLK)

        @pl.when(spot < CHIPS)
        def _():
            high[:, at], low[:, at] = split(root[:, pl.ds(pl.multiple_of(spot * BLK, BLK), BLK)])

        @pl.when(spot >= CHIPS)
        def _():
            block = spot - CHIPS
            columns = pl.ds(pl.multiple_of((block % PER_CORE) * BLK, BLK), BLK)
            ours = block // PER_CORE == core[0]
            high[:, at], low[:, at] = split(jnp.where(ours, mine[:, columns], theirs[:, columns]))


def pick(spots, core, root, cross, cross_theirs):
    shape = jax.ShapeDtypeStruct((root.shape[0], spots.shape[0] * BLK), jnp.bfloat16)
    space = pl.BlockSpec(memory_space=pltpu.VMEM)
    scalars = [pl.BlockSpec(memory_space=pltpu.SMEM)] * 2
    return pl.pallas_call(
        pick_kernel,
        in_specs=scalars + [space] * 3,
        out_specs=[space] * 2,
        out_shape=[shape] * 2,
        compiler_params=pltpu.CompilerParams(vmem_limit_bytes=VMEM_LIMIT),
        cost_estimate=pl.CostEstimate(flops=0, bytes_accessed=20 * root.size, transcendentals=0),
    )(spots, core, root, cross, cross_theirs)


def halves_of(out, core, keep, give):
    rows = keep.shape[1]
    for ref, half in ((keep, core), (give, 1 - core)):
        for k in range(ref.shape[0]):
            ref[k] = out[pl.ds(pl.multiple_of(half * rows, rows), rows), k * LANES:(k + 1) * LANES]


def column_kernel(spots, core, top_high, top_low, *refs):
    step = pl.program_id(0)
    lefts, (lower, out_top, out_low, keep, give, high, low) = refs[:4 * GROUP], refs[4 * GROUP:]
    turned_high, turned_low, inners, inner_others = [lefts[kind * GROUP:(kind + 1) * GROUP] for kind in range(4)]
    top = out_top.shape[0]
    high[:top, :], low[:top, :] = top_high[...], top_low[...]

    for q in range(GROUP):
        spot, at = spots[step * GROUP + q], q * BLK

        @pl.when(spot < CHIPS)
        def _():
            columns = slice(at, at + BLK)
            high[top:, columns], low[top:, columns] = turned_high[q][...], turned_low[q][...]

        @pl.when(spot >= CHIPS)
        def _():
            ours = (spot - CHIPS) // PER_CORE == core[0]
            columns = slice(at, at + BLK)
            high[top:, columns], low[top:, columns] = split(jnp.where(ours, inners[q][...], inner_others[q][...]))

    for n in range(0, lower.shape[1], 2 * TILE):
        columns = slice(n, n + 2 * TILE)
        total = three_pass(high, low, [lower.at[:, columns]], [lower.shape[0]])

        @pl.when(step == 0)
        def _():
            out_top[:, columns], out_low[:, columns] = -total[:top], -total[top:]

        @pl.when(step > 0)
        def _():
            out_top[:, columns] -= total[:top]
            out_low[:, columns] -= total[top:]

    @pl.when(step == pl.num_programs(0) - 1)
    def _():
        halves_of(out_top, core[0], keep.at[:, :LANES], give.at[:, :LANES])
        halves_of(out_low, core[0], keep.at[:, LANES:], give.at[:, LANES:])


def column_sum(spots, core, picked, turned, inner, inner_theirs, lower):
    top, low, columns = picked[0].shape[0], inner.shape[0], lower.shape[1]

    def listed(shape, place):
        return [
            pl.BlockSpec(shape, functools.partial(lambda q, k, spots, core: place(spots[k * GROUP + q]), q))
            for q in range(GROUP)
        ]

    def block(spot):
        return jnp.maximum(spot - CHIPS, 0) % PER_CORE

    in_specs = [pl.BlockSpec((top, GROUP * BLK), lambda k, spots, core: (0, k))] * 2
    in_specs += 2 * listed((low, BLK), lambda spot: (0, jnp.minimum(spot, CHIPS - 1)))
    in_specs += 2 * listed((low, BLK), lambda spot: (0, block(spot)))
    in_specs.append(pl.BlockSpec((GROUP * BLK, columns), lambda k, spots, core: (k, 0)))
    operands = [x for x in (*turned, inner, inner_theirs) for _ in range(GROUP)]
    shapes = [(top, columns), (low, columns)] + [(columns // LANES, (top + low) // 2, LANES)] * 2
    return pl.pallas_call(
        column_kernel,
        grid_spec=pltpu.PrefetchScalarGridSpec(
            num_scalar_prefetch=2,
            grid=(spots.shape[0] // GROUP,),
            in_specs=in_specs,
            out_specs=[
                pl.BlockSpec(shape, functools.partial(lambda size, k, spots, core: (0,) * size, len(shape)))
                for shape in shapes
            ],
            scratch_shapes=[pltpu.VMEM((top + low, GROUP * BLK), jnp.bfloat16)] * 2,
        ),
        out_shape=[jax.ShapeDtypeStruct(shape, jnp.float32) for shape in shapes],
        compiler_params=pltpu.CompilerParams(vmem_limit_bytes=VMEM_LIMIT),
        cost_estimate=pl.CostEstimate(flops=1000, bytes_accessed=1000, transcendentals=0),
    )(spots, core, *picked, *operands, lower)


def last_kernel(spots, core, mine, theirs, lower, base, out, high, low):
    @pl.when(pl.program_id(0) == 0)
    def _():
        is_first = core[0] == 0
        for j in range(spots.shape[0]):
            spot = spots[j]
            chip, first_low = jnp.minimum(spot, CHIPS - 1), jnp.maximum(2 * (spot - CHIPS), 0)
            parts = in_order(is_first, mine[chip, :LANES, :], theirs[chip, :LANES, :])
            for half, value in enumerate(parts):
                c = first_low + half
                lower_rows = jnp.concatenate(in_order(is_first, mine[c, LANES:, :], theirs[c, LANES:, :]))
                at = slice(j * BLK + half * LANES, j * BLK + (half + 1) * LANES)
                high[:, at], low[:, at] = split(jnp.where(spot < CHIPS, value, lower_rows).T)

    out[...] = base[...] - three_pass(high, low, [lower], [lower.shape[0]])


def last_sum(base, mine, theirs, spots, core, lower):
    rows, columns = base.shape
    whole = pl.BlockSpec(mine.shape, lambda n, spots, core: (0, 0, 0))
    tile = pl.BlockSpec((rows, TILE), lambda n, spots, core: (0, n))
    return pl.pallas_call(
        last_kernel,
        grid_spec=pltpu.PrefetchScalarGridSpec(
            num_scalar_prefetch=2,
            grid=(columns // TILE,),
            in_specs=[whole, whole, pl.BlockSpec((lower.shape[0], TILE), lambda n, spots, core: (0, n)), tile],
            out_specs=tile,
            scratch_shapes=[pltpu.VMEM((rows, lower.shape[0]), jnp.bfloat16)] * 2,
        ),
        out_shape=jax.ShapeDtypeStruct(base.shape, jnp.float32),
        compiler_params=pltpu.CompilerParams(vmem_limit_bytes=VMEM_LIMIT),
        cost_estimate=pl.CostEstimate(flops=1000, bytes_accessed=1000, transcendentals=0),
    )(spots, core, mine, theirs, lower, base)


def after(value, *others):
    return lax.optimization_barrier((value,) + others)[0]


def pull(value, way):
    pairs = []
    for target in range(CHIPS):
        y, x = divmod(target, SIDE)
        pairs.append((((y + way[0]) % SIDE) * SIDE + (x + way[1]) % SIDE, target))
    return lax.ppermute(value, "row", pairs)


def other_core(value):
    return lax.ppermute(value, "col", [(0, 1), (1, 0)])


def turn(core, keep, give):
    sent = jnp.concatenate(in_order(core == 0, keep, other_core(give)), axis=0)
    return lax.all_to_all(sent, "row", split_axis=0, concat_axis=0, tiled=True)


def first_round(own):
    return [pull(own, way) for way in (EAST, WEST, SOUTH, NORTH)]


def second_round(near, *gates):
    e, w, s, n = near
    es = pull(after(s, e, *gates), EAST)
    wn = pull(after(n, w, *gates), WEST)
    sw = pull(after(w, s, *gates), SOUTH)
    ne = pull(after(e, n, *gates), NORTH)
    return es, wn, sw, ne


def third_round(diagonal, *gates):
    es, wn, sw, ne = diagonal
    ees = pull(after(es, *gates), EAST)
    wwn = pull(after(wn, *gates), WEST)
    sse = pull(after(es, sw, *gates), SOUTH)
    nnw = pull(after(wn, ne, *gates), NORTH)
    return ees, wwn, sse, nnw


def fourth_round(near, third, *gates):
    e, w, s, n = near
    ees, wwn, sse, nnw = third
    half = e.shape[0] // 2
    first = pull(after(nnw[:half], wwn, *gates), WEST)
    second = pull(after(wwn[half:], nnw, *gates), NORTH)
    return pull(after(e, ees, *gates), EAST), pull(after(s, sse, *gates), SOUTH), first, second


PLACES = [
    [(0, 0), EAST, WEST, SOUTH, NORTH, (1, 1), (3, 3), (1, 3), (3, 1)],
    [(1, 2), (3, 2), (2, 1), (2, 3)],
    [(0, 2), (2, 0), (2, 2), (2, 2)],
]
WHOLE = (0, 1)
HALVES = [[WHOLE] * 9, [WHOLE] * 4, [WHOLE, WHOLE, (0,), (1,)]]


def body(root_inverse, panel_one, diag_one, panel_two, diag_two, structure):
    place = lax.axis_index("row")
    core = lax.axis_index("col").astype(jnp.int32)
    core_vector = core[None]
    blocks = structure[0, 0]
    own_upper, own_lower = panel_one[0], panel_two[0, 0]

    def chips(places):
        down = jnp.array([spot[0] for spot in places], jnp.int32)
        right = jnp.array([spot[1] for spot in places], jnp.int32)
        return ((place // SIDE + down) % SIDE) * SIDE + (place % SIDE + right) % SIDE

    halves = sum(HALVES, [])
    every_spots = chips(sum(PLACES, []))
    far_spots = chips(PLACES[2][2:]) * 2 + jnp.arange(2, dtype=jnp.int32)

    root_rows = lax.all_gather(root_inverse, ("leaf", "col"), axis=1, tiled=True)

    near = first_round(own_upper)
    diagonal = second_round(near)
    third = third_round(diagonal)
    lower = lax.all_gather(after(own_lower, *near), "row", axis=0, tiled=True)
    early = [own_upper, *near, *diagonal]
    cross, = cross_sum(None, root_rows, every_spots[:9], core_vector, early)
    fourth = fourth_round(near, third)
    third_spots = jnp.concatenate([every_spots[9:13], far_spots])
    cross, = cross_sum(cross, root_rows, third_spots, core_vector, [*third, *fourth[2:]])
    cross, keep, give = cross_sum(cross, root_rows, every_spots[13:15], core_vector, fourth[:2], True)
    turned = turn(core, keep, give)
    picked = pick(blocks, core_vector, root_rows, cross, other_core(cross))
    turned = after(turned, *picked)
    turned_theirs = other_core(turned)
    upper = [*early, *third, *fourth]
    inner, turned_parts = inner_sum(diag_one[0], turned, turned_theirs, every_spots, core_vector, sum(HALVES, []), upper)

    top, low, keep, give = column_sum(
        blocks, core_vector, picked, turned_parts, inner, other_core(inner), lower
    )
    turned = turn(core, keep, give)
    inner_low = last_sum(diag_two[0, 0], turned, other_core(turned), blocks, core_vector, lower)
    return cross[None], inner[None], top[None, None], low[None, None], inner_low[None, None]


def solution(mesh):
    in_specs = (
        P("row", ("leaf", "col")),
        P("leaf", "row", "col"),
        P("leaf", "row", "col"),
        P("leaf", None, "row", "col"),
        P("leaf", None, "row", "col"),
        P("leaf", None, None),
    )
    out_specs = (
        P("leaf", "row", "col"),
        P("leaf", "row", "col"),
        P("leaf", None, "row", "col"),
        P("leaf", None, "row", "col"),
        P("leaf", None, "row", "col"),
    )
    return jax.shard_map(body, mesh=mesh, in_specs=in_specs, out_specs=out_specs, check_vma=False)
```
